128 devices in a mesh: cfg: 2 (over core), seq: 64 (over z, y, x).
Axes of the slice: x: 4, y: 4, z: 4, core: 2. Of those that a mesh axis runs over, the one named last changes fastest.
Arguments:
- queries: bfloat16 [2, 49152, 2560], P('cfg', 'seq'), may hold values from -48 to 48
- keys: bfloat16 [2, 49152, 2560], P('cfg', 'seq'), may hold values from -11 to 11
- values: bfloat16 [2, 49152, 2560], P('cfg', 'seq'), may hold values from -6 to 6
- tile_lists: int32 [2, 768, 16], P('cfg', 'seq'), may hold values from -1 to 767, as said below
- tile_order: int32 [768], replicated, may hold values from 0 to 767, as said below
Outputs:
- guided: float32 [49152, 2560], P('seq', 'cfg')
The draws below stay inside these ranges and needn't reach their ends.
Inputs may be any that keep to these rules, and one draw needn't show every extreme that they name: `tile_lists`: entry 0 of each list is the query tile itself; entries -1 are empty and come last; the named tiles of one list are distinct. For each pass, the tiles named by the lists of the query tiles on one index d of seq lie on indices d - 2 to d + 2, and at most 4 of them on any one index other than d; in every draw some index names exactly 4 tiles of a neighbour. `tile_order`: A permutation of the video tiles.
All inputs are finite; a program needn't handle non-finite values.
Results may differ from the reference program's by a relative error of at most 0.0022.
Values may be sent and summed in bfloat16 or wider, within the bound.
No kernel may reach another device: no remote copies, remote signals or barrier semaphores. Data moves between devices by JAX's collectives and lax.ppermute only.
A program may use at most 192 MiB of HBM per device.

```python
import jax
import jax.numpy as jnp
import numpy as np
from jax import lax

HEADS = 20
HD = 128
TILE = 64
TILES_DEV = 12
TOPK = 16
RADIUS = 2
CAP = 4
TILES = 768
TOKENS = 49152
WIDTH = 2560


def permute_each(key, count, length):
    return jax.vmap(lambda single: jax.random.permutation(single, length))(jax.random.split(key, count))


def pass_lists(key):
    devices = TILES // TILES_DEV
    reaches = 2 * RADIUS
    distance = jnp.asarray(np.concatenate([np.arange(-RADIUS, 0), np.arange(1, RADIUS + 1)]), jnp.int32)
    subkeys = jax.random.split(key, 6)
    device = jnp.arange(devices, dtype=jnp.int32)[:, None]
    counts = jax.random.randint(subkeys[0], (devices, reaches), 1, CAP + 1)
    phase = jax.random.randint(subkeys[1], (), 0, 3)
    forced = ((device + phase) % 3 == 0) & (distance[None, :] == 1)
    counts = jnp.where(forced, CAP, counts)
    target = device + distance[None, :]
    counts = jnp.where((target >= 0) & (target < devices), counts, 0)
    picked = permute_each(subkeys[2], devices * reaches, TILES_DEV).reshape(devices, reaches, TILES_DEV)[:, :, :CAP]
    living = jnp.arange(CAP)[None, None, :] < counts[:, :, None]
    remote = jnp.where(living, target[:, :, None] * TILES_DEV + picked, -1).reshape(devices, reaches * CAP)
    shuffle = permute_each(subkeys[3], devices, reaches * CAP)
    remote_rank = jnp.where(remote >= 0, shuffle, shuffle + reaches * CAP)
    remote = jnp.take_along_axis(remote, jnp.argsort(remote_rank, axis=1), axis=1)
    own_order = permute_each(subkeys[4], devices, TILES_DEV)
    local_ids = jnp.arange(TILES_DEV, dtype=jnp.int32)
    others = jnp.where(own_order[:, None, :] == local_ids[None, :, None], -1, device[:, :, None] * TILES_DEV + own_order[:, None, :])
    sequence = jnp.concatenate([jnp.broadcast_to(remote[:, None, :], (devices, TILES_DEV, reaches * CAP)), others], axis=2)
    ordering = jnp.argsort((sequence < 0).astype(jnp.int32), axis=2, stable=True)
    sequence = jnp.take_along_axis(sequence, ordering, axis=2)
    length = jnp.sum((sequence >= 0).astype(jnp.int32), axis=2)
    rotation = permute_each(subkeys[5], devices, TILES_DEV)
    beginning = rotation * (TOPK - 1)
    within = jnp.arange(TOPK - 1, dtype=jnp.int32)
    location = (beginning[:, :, None] + within[None, None, :]) % length[:, :, None]
    chosen = jnp.take_along_axis(sequence, location, axis=2)
    chosen = jnp.where(within[None, None, :] < length[:, :, None], chosen, -1)
    itself = device * TILES_DEV + local_ids[None, :]
    return jnp.concatenate([itself[:, :, None], chosen], axis=2).reshape(TILES, TOPK)


def tile_plan(key):
    storage = jax.random.permutation(jax.random.fold_in(key, 11), TILES).astype(jnp.int32)
    slots = jnp.stack([pass_lists(jax.random.fold_in(key, 20)), pass_lists(jax.random.fold_in(key, 21))])
    listed = jnp.where(slots >= 0, storage[jnp.maximum(slots, 0)], -1)
    return (storage, listed.astype(jnp.int32))


def anchor_rows(key):
    return jnp.clip(jax.random.normal(jax.random.fold_in(key, 31), (2, TOKENS, HEADS * HD), jnp.float32), -4.0, 4.0)


def draw_tile_lists(key, part):
    storage, listed = tile_plan(key)
    return listed


def draw_tile_order(key, part):
    storage, listed = tile_plan(key)
    return storage


def draw_keys(key, part):
    anchor = anchor_rows(key)
    return anchor.astype(jnp.bfloat16)


def draw_queries(key, part):
    anchor = anchor_rows(key)
    key = jax.random.fold_in(key, 9)
    return (1.5 * jnp.clip(jax.random.normal(key, anchor.shape, jnp.float32), -4.0, 4.0)).astype(jnp.bfloat16)


def steps_of(rng, shape, cuts, smallest, high):
    factor_of, own = 1.0, jax.random.fold_in(rng, 6)
    for axis_at, parts in cuts:
        steps = jnp.exp(jax.random.uniform(jax.random.fold_in(own, axis_at), (parts,), jnp.float32, smallest / len(cuts), high / len(cuts)))
        factor_of = factor_of * jnp.repeat(steps, shape[axis_at] // parts).reshape([-1 if axis == axis_at else 1 for axis in range(len(shape))])
    return factor_of


def centred(own_key, shape, scale, bound, pieces=(), kind=jnp.bfloat16):
    gain = steps_of(own_key, shape, pieces, -0.22, 0.18) if pieces else 1.0
    result = jax.random.normal(own_key, shape, jnp.float32) * scale * gain
    return jnp.minimum(jnp.maximum(result, -bound), bound).astype(kind)


def setup_inputs(seed: int = 0) -> dict:
    seeds = jax.random.split(jax.random.key(seed), 6)
    return {
        "queries": draw_queries(jax.random.fold_in(seeds[5], 71), 0),
        "keys": draw_keys(jax.random.fold_in(seeds[5], 71), 0),
        "values": centred(seeds[2], (2, TOKENS, WIDTH), 1.0, 6.0, ((0, 2), (1, 64))),
        "tile_lists": draw_tile_lists(jax.random.fold_in(seeds[5], 71), 0),
        "tile_order": draw_tile_order(jax.random.fold_in(seeds[5], 71), 0),
    }


guidance_scale = 5.0


def attend_pass(query_rows, key_rows, value_rows, listed, slot_of):
    query_tiles = query_rows.reshape(TILES, TILE, HEADS, HD)
    key_tiles = key_rows.reshape(TILES, TILE, HEADS, HD)
    value_tiles = value_rows.reshape(TILES, TILE, HEADS, HD)

    def one_tile(item):
        query_tile, entries = item
        present = entries >= 0
        picks = jnp.where(present, slot_of[jnp.maximum(entries, 0)], 0).astype(jnp.int32)
        chosen_keys = key_tiles[picks].reshape(TOPK * TILE, HEADS, HD).astype(jnp.float32)
        chosen_values = value_tiles[picks].reshape(TOPK * TILE, HEADS, HD).astype(jnp.float32)
        scores = jnp.einsum("qhd,khd->hqk", query_tile.astype(jnp.float32), chosen_keys,
                            precision=lax.Precision.HIGHEST) * (HD ** -0.5)
        allowed = jnp.repeat(present, TILE)[None, None, :]
        scores = jnp.where(allowed, scores, -1e30)
        largest = jnp.max(scores, axis=-1, keepdims=True)
        weights = jnp.where(allowed, jnp.exp(scores - largest), 0.0)
        totals = jnp.sum(weights, axis=-1)
        rounded = lax.optimization_barrier(weights.astype(jnp.bfloat16)).astype(jnp.float32)
        mixed = jnp.einsum("hqk,khd->qhd", rounded, chosen_values, precision=lax.Precision.HIGHEST)
        return (mixed / jnp.transpose(totals)[:, :, None]).reshape(TILE, HEADS * HD)

    return lax.map(one_tile, (query_tiles, listed)).reshape(TOKENS, HEADS * HD)


def reference(queries, keys, values, tile_lists, tile_order):
    slot_of = jnp.zeros((TILES,), jnp.int32).at[tile_order].set(jnp.arange(TILES, dtype=jnp.int32))
    conditional = attend_pass(queries[0], keys[0], values[0], tile_lists[0], slot_of)
    unconditional = attend_pass(queries[1], keys[1], values[1], tile_lists[1], slot_of)
    return unconditional + guidance_scale * (conditional - unconditional)
```

```python
import functools

import jax
import jax.numpy as jnp
from jax import lax
from jax.experimental import pallas as pl
from jax.experimental.pallas import tpu as pltpu
from jax.sharding import PartitionSpec as P

HD = 128
CAP = 4
GROUP = 4
REACHES = (1, -1, 2, -2)
HANDED = ((0, 6), (6, 4))
KEPT = ((0, 6), (6, 4))
guidance_scale = 5.0
ANY = pl.BlockSpec(memory_space=pl.ANY)
SMEM = pl.BlockSpec(memory_space=pltpu.SMEM)
VMEM = pl.BlockSpec(memory_space=pltpu.VMEM)
SHORT = pl.CostEstimate(flops=1, bytes_accessed=1, transcendentals=0)
PARAMS = pltpu.CompilerParams(vmem_limit_bytes=63 * 1024 * 1024)


def shifted(value, axis, steps):
    count = lax.axis_size(axis)
    initial, last = (max(0, -steps), min(count, count - steps))
    return lax.ppermute(value, axis, [(source, source + steps) for source in range(initial, last)])


def any_equal(listed, tile_id):
    return jnp.max((listed == tile_id).astype(jnp.int32))


def pack(tile, start, picks, keys, values, outs, pools, load_sems, sems, plan=None, wait=True):
    width = pools.shape[2]
    columns = pl.ds(pl.multiple_of(start, HD), width)
    loads = [
        pltpu.make_async_copy(source.at[:, columns], pools.at[kind], load_sems.at[kind])
        for kind, source in enumerate((keys, values))
    ]
    for copy in loads:
        copy.start()
    if plan is not None:
        plan()
    copies = []
    for kind in range(2):
        loads[kind].wait()
        for reach in range(len(outs)):
            for entry in range(CAP):
                first = pl.multiple_of(picks[reach, entry] * tile, tile)
                copy = pltpu.make_async_copy(
                    pools.at[kind, pl.ds(first, tile), :],
                    outs[reach].at[kind, pl.ds(entry * tile, tile), :],
                    sems.at[len(copies)],
                )
                copy.start()
                copies.append(copy)
    if wait:
        for copy in copies:
            copy.wait()
    return copies


def first_pack_kernel(tile, tiles_here, place, order, *refs):
    listed = refs[:2]
    keys, values = refs[2:4]
    outs = refs[-7:-5]
    picks_out, picks, pools, load_sems, sems = refs[-5:]
    base = place[0] * tiles_here

    def plan():
        for reach in range(2):
            wanted = listed[reach][...]
            filled = jnp.int32(0)
            for entry in range(CAP):
                picks[reach, entry] = 0
            for slot in range(tiles_here):
                picks[reach, filled] = slot
                filled = jnp.minimum(filled + any_equal(wanted, order[base + slot]), CAP)
            for entry in range(CAP):
                picks_out[reach, entry] = picks[reach, entry]

    pack(tile, place[1], picks, keys, values, outs, pools, load_sems, sems, plan)


def later_pack_kernel(tile, count, place, near, far, keys, values, *refs):
    class Picks:
        def __getitem__(self, at):
            return (near if at[0] < 2 else far)[at[0] % 2, at[1]]

    outs, scratch = refs[-(len(REACHES) + 3) * count : -3 * count], refs[-3 * count :]
    waits = []
    for chunk in range(count):
        mine = outs[len(REACHES) * chunk : len(REACHES) * (chunk + 1)]
        waits += pack(tile, place[chunk], Picks(), keys, values, mine, *scratch[3 * chunk : 3 * chunk + 3], wait=False)
    for copy in waits:
        copy.wait()


def index_kernel(tiles_here, devices, place, order, listed_ref, index_ref):
    listed = listed_ref[...]
    here = place[0]
    index = jnp.zeros_like(listed)
    for slot in range(tiles_here):
        index = jnp.where(listed == order[here * tiles_here + slot], slot, index)
    for reach, distance in enumerate(REACHES):
        there = here + distance
        inside = jnp.logical_and(there >= 0, there < devices)
        base = jnp.where(inside, there, here) * tiles_here
        filled = jnp.int32(0)
        for slot in range(tiles_here):
            tile_id = jnp.where(inside, order[base + slot], -2)
            index = jnp.where(listed == tile_id, tiles_here + CAP * reach + filled, index)
            filled = jnp.minimum(filled + any_equal(listed, tile_id), CAP - 1)
    index_ref[...] = index


def attend_kernel(heads, tile, tiles_here, topk, kept, place, index, counts, queries, keys, values, *refs):
    arrived = refs[: len(REACHES)]
    rest = refs[len(REACHES) :]
    out, q_pool, k_pool, v_pool, scores, tops, result, other_pool, in_sems, out_sems = rest[-10:]
    width = heads * HD
    rows = tile * tiles_here
    columns = pl.ds(pl.multiple_of(place[1], HD), width)
    copies = [pltpu.make_async_copy(queries.at[:, columns], q_pool, in_sems.at[0])]
    for kind, (own, pool) in enumerate(((keys, k_pool), (values, v_pool))):
        copies.append(pltpu.make_async_copy(own.at[:, columns], pool.at[pl.ds(0, rows), :], in_sems.at[len(copies)]))
        for reach in range(len(REACHES)):
            copies.append(
                pltpu.make_async_copy(
                    arrived[reach].at[kind],
                    pool.at[pl.ds(rows + reach * CAP * tile, CAP * tile), :],
                    in_sems.at[len(copies)],
                )
            )
    before_scores = 2 + len(REACHES)
    if kept is not None:
        for piece, (to, source, count) in enumerate(kept[1:]):
            copies.append(
                pltpu.make_async_copy(
                    rest[piece].at[:, pl.ds(source, count)],
                    other_pool.at[:, pl.ds(to, count)],
                    in_sems.at[len(copies)],
                )
            )
        out = out.at[:, pl.ds(kept[0], width)]
    for copy in copies:
        copy.start()
    factor = HD ** (-0.5) * 1.4426950408889634
    side = place[0]
    span = GROUP * tile
    groups = topk // GROUP
    zeros = jnp.zeros((tile, HD), jnp.bfloat16)

    def rows_of(i):
        return pl.ds(pl.multiple_of(i * tile, tile), tile)

    def gathered(pool, i, group, pair):
        picks = [pl.multiple_of(index[i, group * GROUP + j] * tile, tile) for j in range(GROUP)]
        return jnp.concatenate([pool[pl.ds(p, tile), pair * 2 * HD : (pair + 1) * 2 * HD] for p in picks], axis=0)

    def score(i, slot):
        for pair in range(heads // 2):
            lanes = [slice((2 * pair + j) * HD, (2 * pair + j + 1) * HD) for j in range(2)]
            query = jnp.concatenate(
                [
                    jnp.concatenate([q_pool[rows_of(i), lanes[0]], zeros], axis=1),
                    jnp.concatenate([zeros, q_pool[rows_of(i), lanes[1]]], axis=1),
                ],
                axis=0,
            )
            top = jnp.full((2 * tile, HD), -jnp.inf, jnp.float32)
            for group in range(groups):
                part = lax.dot_general(
                    query,
                    gathered(k_pool, i, group, pair),
                    (((1,), (1,)), ((), ())),
                    preferred_element_type=jnp.float32,
                )
                place_of = lax.broadcasted_iota(jnp.int32, (1, span), 1) + group * span
                part = jnp.where(place_of < counts[i] * tile, part, -1e30)
                scores[slot, pair, :, group * span : (group + 1) * span] = part
                for j in range(span // HD):
                    top = jnp.maximum(top, part[:, j * HD : (j + 1) * HD])
            tops[slot, pair] = jnp.broadcast_to(jnp.max(top, axis=1, keepdims=True), top.shape)

    def mix(i, slot):
        for pair in range(heads // 2):
            top = tops[slot, pair]
            total = jnp.zeros((2 * tile, HD), jnp.float32)
            mixed = [jnp.zeros((tile, HD), jnp.float32)] * 2
            for group in range(groups):
                rounded = []
                for j in range(span // HD):
                    first = group * span + j * HD
                    weights = jnp.exp2((scores[slot, pair, :, first : first + HD] - top) * factor)
                    total = total + weights
                    rounded.append(weights.astype(jnp.bfloat16))
                both = jnp.dot(
                    jnp.concatenate(rounded, axis=1),
                    gathered(v_pool, i, group, pair),
                    preferred_element_type=jnp.float32,
                )
                mixed = [mixed[0] + both[:tile, :HD], mixed[1] + both[tile:, HD:]]
            total = jnp.sum(total, axis=1, keepdims=True)
            for j in range(2):
                lanes = slice((2 * pair + j) * HD, (2 * pair + j + 1) * HD)
                attended = mixed[j] / total[j * tile : (j + 1) * tile]
                if kept is not None:
                    other = other_pool[rows_of(i), lanes]
                    conditional = jnp.where(side == 0, attended, other)
                    unconditional = jnp.where(side == 0, other, attended)
                    attended = unconditional + guidance_scale * (conditional - unconditional)
                result[rows_of(i), lanes] = attended

    def copy_out(step):
        here = pl.ds(pl.multiple_of(step * 2 * tile, 2 * tile), 2 * tile)
        return pltpu.make_async_copy(result.at[here, :], out.at[here, :], out_sems.at[step])

    for copy in copies[:before_scores]:
        copy.wait()
    score(0, 0)
    for copy in copies[before_scores:]:
        copy.wait()

    def two_tiles(step, carry):
        i = step * 2
        score(i + 1, 1)
        mix(i, 0)
        score(jnp.minimum(i + 2, tiles_here - 1), 0)
        mix(i + 1, 1)
        copy_out(step).start()
        return carry

    lax.fori_loop(0, tiles_here // 2, two_tiles, 0)
    for step in range(tiles_here // 2):
        copy_out(step).wait()


def per_device(queries, keys, values, tile_lists, tile_order):
    queries, keys, values, listed = queries[0], keys[0], values[0], tile_lists[0]
    tiles_here, topk = listed.shape
    rows, features = queries.shape
    tile = rows // tiles_here
    devices = lax.axis_size("seq")
    side, position = lax.axis_index("cfg"), lax.axis_index("seq")
    half = features // 2
    neighbours = len(REACHES)
    chunks = []
    for kept, parts, first in ((False, HANDED, (1 - side) * half), (True, KEPT, side * half)):
        for head, heads in parts:
            chunks.append((kept, head, heads, (first + head * HD).astype(jnp.int32)))

    asked = [shifted(listed, "seq", distance) for distance in REACHES]

    def buffers(chunk, count):
        width = chunks[chunk][2] * HD
        return [jax.ShapeDtypeStruct((2, CAP * tile, width), keys.dtype)] * count

    def pools(chunk, count):
        width = chunks[chunk][2] * HD
        return [
            pltpu.VMEM((2, rows, width), keys.dtype),
            pltpu.SemaphoreType.DMA((2,)),
            pltpu.SemaphoreType.DMA((2 * count * CAP,)),
        ]

    def first_pack(lists, after):
        table = jax.ShapeDtypeStruct((2, CAP + 4), jnp.int32)
        return pl.pallas_call(
            functools.partial(first_pack_kernel, tile, tiles_here),
            out_shape=buffers(0, 2) + [table],
            in_specs=[SMEM, SMEM, VMEM, VMEM] + [ANY] * (2 + len(after)),
            out_specs=[ANY, ANY, SMEM],
            scratch_shapes=[pltpu.SMEM(table.shape, jnp.int32)] + pools(0, 2),
            compiler_params=PARAMS,
            cost_estimate=SHORT,
            name="first_pack",
        )(jnp.stack([position, chunks[0][3]]).astype(jnp.int32), tile_order, *lists, keys, values, *after)

    def later_pack(picks, after):
        later = range(1, len(chunks))
        made = pl.pallas_call(
            functools.partial(later_pack_kernel, tile, len(later)),
            out_shape=sum([buffers(chunk, neighbours) for chunk in later], []),
            in_specs=[SMEM, SMEM, SMEM, ANY, ANY] + [ANY] * len(after),
            out_specs=[ANY] * (neighbours * len(later)),
            scratch_shapes=sum([pools(chunk, neighbours) for chunk in later], []),
            compiler_params=PARAMS,
            cost_estimate=SHORT,
            name="later_pack",
        )(jnp.stack([chunks[chunk][3] for chunk in later]), *picks, keys, values, *after)
        return [list(made[i : i + neighbours]) for i in range(0, len(made), neighbours)]

    def moved(sending):
        return [shifted(buffer, "seq", -distance) for buffer, distance in zip(sending, REACHES)]

    index = pl.pallas_call(
        functools.partial(index_kernel, tiles_here, devices),
        out_shape=jax.ShapeDtypeStruct(listed.shape, jnp.int32),
        in_specs=[SMEM, SMEM, VMEM],
        out_specs=VMEM,
        compiler_params=PARAMS,
        cost_estimate=SHORT,
        name="pool_index",
    )(position.astype(jnp.int32)[None], tile_order, listed)
    counts = jnp.sum((listed >= 0).astype(jnp.int32), axis=1)

    *near, near_picks = first_pack(asked[:2], [])
    *far, far_picks = first_pack(asked[2:], near[:1])
    arrived = [moved(near + far)]
    arrived += [moved(sending) for sending in later_pack([near_picks, far_picks], [arrived[0][2], index])]
    partners, guided, result = [], None, None
    pool = tiles_here * tile + neighbours * CAP * tile
    for chunk, (kept, head, heads, start) in enumerate(chunks):
        width = heads * HD
        operands = [jnp.stack([side, start]).astype(jnp.int32), index, counts, queries, keys, values]
        operands += arrived[chunk]
        aliases, columns = {}, None
        if kept:
            columns = [head * HD]
            for handed_head, handed_heads, partner in partners:
                first, last = max(head, handed_head), min(head + heads, handed_head + handed_heads)
                if first < last:
                    operands.append(partner)
                    columns.append(((first - head) * HD, (first - handed_head) * HD, (last - first) * HD))
        if guided is None and result is not None:
            operands.append(result)
        if guided is not None:
            aliases = {len(operands): 0}
            operands.append(guided)
        out_shape = jax.ShapeDtypeStruct((rows, half if kept else width), jnp.float32)
        result = pl.pallas_call(
            functools.partial(attend_kernel, heads, tile, tiles_here, topk, columns),
            out_shape=out_shape,
            in_specs=[SMEM] * 3 + [ANY] * (len(operands) - 3),
            out_specs=ANY,
            input_output_aliases=aliases,
            scratch_shapes=[
                pltpu.VMEM((rows, width), jnp.bfloat16),
                pltpu.VMEM((pool, width), jnp.bfloat16),
                pltpu.VMEM((pool, width), jnp.bfloat16),
                pltpu.VMEM((2, heads // 2, 2 * tile, topk * tile), jnp.float32),
                pltpu.VMEM((2, heads // 2, 2 * tile, HD), jnp.float32),
                pltpu.VMEM((rows, width), jnp.float32),
                pltpu.VMEM((rows, width) if kept else (8, HD), jnp.float32),
                pltpu.SemaphoreType.DMA((16,)),
                pltpu.SemaphoreType.DMA((tiles_here // 2,)),
            ],
            compiler_params=PARAMS,
            cost_estimate=pl.CostEstimate(
                flops=10000 * rows * topk * tile * width,
                bytes_accessed=100000 * rows * width,
                transcendentals=rows * topk * tile * heads,
            ),
            name=("guide_" if kept else "attend_") + str(chunk),
        )(*operands)
        if kept:
            guided = result
        else:
            partners.append((head, heads, lax.ppermute(result, "cfg", [(0, 1), (1, 0)])))
    return guided


def solution(mesh):
    return jax.shard_map(
        per_device,
        mesh=mesh,
        in_specs=(
            P("cfg", "seq", None),
            P("cfg", "seq", None),
            P("cfg", "seq", None),
            P("cfg", "seq", None),
            P(),
        ),
        out_specs=P("seq", "cfg"),
        check_vma=False,
    )
```

```python
import functools

import jax
import jax.numpy as jnp
from jax import lax
from jax.experimental import pallas as pl
from jax.experimental.pallas import tpu as pltpu
from jax.sharding import PartitionSpec as P

HD = 128
CAP = 4
GROUP = 4
REACHES = (1, -1, 2, -2)
HANDED = ((0, 6), (6, 4))
KEPT = ((0, 6), (6, 4))
guidance_scale = 5.0
ANY = pl.BlockSpec(memory_space=pl.ANY)
SMEM = pl.BlockSpec(memory_space=pltpu.SMEM)
VMEM = pl.BlockSpec(memory_space=pltpu.VMEM)
LONG = pl.CostEstimate(flops=10**13, bytes_accessed=10**11, transcendentals=0)
SHORT = pl.CostEstimate(flops=1, bytes_accessed=1, transcendentals=0)
PARAMS = pltpu.CompilerParams(vmem_limit_bytes=63 * 1024 * 1024)


def shifted(value, axis, steps):
    count = lax.axis_size(axis)
    initial, last = (max(0, -steps), min(count, count - steps))
    return lax.ppermute(value, axis, [(source, source + steps) for source in range(initial, last)])


def any_equal(listed, tile_id):
    return jnp.max((listed == tile_id).astype(jnp.int32))


def pack(tile, start, picks, keys, values, outs, pools, load_sems, sems, plan=None, wait=True):
    width = pools.shape[2]
    columns = pl.ds(pl.multiple_of(start, HD), width)
    loads = [
        pltpu.make_async_copy(source.at[:, columns], pools.at[kind], load_sems.at[kind])
        for kind, source in enumerate((keys, values))
    ]
    for copy in loads:
        copy.start()
    if plan is not None:
        plan()
    copies = []
    for kind in range(2):
        loads[kind].wait()
        for reach in range(len(outs)):
            for entry in range(CAP):
                first = pl.multiple_of(picks[reach, entry] * tile, tile)
                copy = pltpu.make_async_copy(
                    pools.at[kind, pl.ds(first, tile), :],
                    outs[reach].at[kind, pl.ds(entry * tile, tile), :],
                    sems.at[len(copies)],
                )
                copy.start()
                copies.append(copy)
    if wait:
        for copy in copies:
            copy.wait()
    return copies


def first_pack_kernel(tile, tiles_here, place, order, *refs):
    listed = refs[: len(REACHES)]
    keys, values = refs[len(REACHES) : len(REACHES) + 2]
    outs = refs[-5 - len(REACHES) : -5]
    picks_out, picks, pools, load_sems, sems = refs[-5:]
    base = place[0] * tiles_here

    def plan():
        for reach in range(len(REACHES)):
            wanted = listed[reach][...]
            counts = []
            for first in range(0, tiles_here, 6):
                packed = jnp.zeros(wanted.shape, jnp.float32)
                for slot in range(first, first + 6):
                    packed = jnp.where(wanted == order[base + slot], float(16 ** (slot - first)), packed)
                total = jnp.sum(packed).astype(jnp.int32)
                counts += [(total >> (4 * j)) & 15 for j in range(6)]
            filled = jnp.int32(0)
            for entry in range(CAP):
                picks[reach, entry] = 0
            for slot in range(tiles_here):
                picks[reach, filled] = slot
                filled = jnp.minimum(filled + jnp.minimum(counts[slot], 1), CAP)
            for entry in range(CAP):
                picks_out[reach, entry] = picks[reach, entry]

    pack(tile, place[1], picks, keys, values, outs, pools, load_sems, sems, plan)


def later_pack_kernel(tile, count, place, picks, keys, values, *refs):
    outs, scratch = refs[-(len(REACHES) + 3) * count : -3 * count], refs[-3 * count :]
    waits = []
    for chunk in range(count):
        mine = outs[len(REACHES) * chunk : len(REACHES) * (chunk + 1)]
        waits += pack(tile, place[chunk], picks, keys, values, mine, *scratch[3 * chunk : 3 * chunk + 3], wait=False)
    for copy in waits:
        copy.wait()


def index_kernel(tiles_here, devices, place, order, listed_ref, index_ref):
    listed = listed_ref[...]
    here = place[0]
    index = jnp.zeros_like(listed)
    for slot in range(tiles_here):
        index = jnp.where(listed == order[here * tiles_here + slot], slot, index)
    for reach, distance in enumerate(REACHES):
        there = here + distance
        inside = jnp.logical_and(there >= 0, there < devices)
        base = jnp.where(inside, there, here) * tiles_here
        filled = jnp.int32(0)
        for slot in range(tiles_here):
            tile_id = jnp.where(inside, order[base + slot], -2)
            index = jnp.where(listed == tile_id, tiles_here + CAP * reach + filled, index)
            filled = jnp.minimum(filled + any_equal(listed, tile_id), CAP - 1)
    index_ref[...] = index


def attend_kernel(heads, tile, tiles_here, topk, kept, place, index, counts, queries, keys, values, *refs):
    arrived = refs[: len(REACHES)]
    rest = refs[len(REACHES) :]
    out, q_pool, k_pool, v_pool, scores, tops, result, other_pool, in_sems, out_sems = rest[-10:]
    width = heads * HD
    rows = tile * tiles_here
    columns = pl.ds(pl.multiple_of(place[1], HD), width)
    copies = [pltpu.make_async_copy(queries.at[:, columns], q_pool, in_sems.at[0])]
    for kind, (own, pool) in enumerate(((keys, k_pool), (values, v_pool))):
        copies.append(pltpu.make_async_copy(own.at[:, columns], pool.at[pl.ds(0, rows), :], in_sems.at[len(copies)]))
        for reach in range(len(REACHES)):
            copies.append(
                pltpu.make_async_copy(
                    arrived[reach].at[kind],
                    pool.at[pl.ds(rows + reach * CAP * tile, CAP * tile), :],
                    in_sems.at[len(copies)],
                )
            )
    before_scores = 2 + len(REACHES)
    if kept is not None:
        for piece, (to, source, count) in enumerate(kept[1:]):
            copies.append(
                pltpu.make_async_copy(
                    rest[piece].at[:, pl.ds(source, count)],
                    other_pool.at[:, pl.ds(to, count)],
                    in_sems.at[len(copies)],
                )
            )
        out = out.at[:, pl.ds(kept[0], width)]
    for copy in copies:
        copy.start()
    factor = HD ** (-0.5) * 1.4426950408889634
    side = place[0]
    span = GROUP * tile
    groups = topk // GROUP
    zeros = jnp.zeros((tile, HD), jnp.bfloat16)

    def rows_of(i):
        return pl.ds(pl.multiple_of(i * tile, tile), tile)

    def gathered(pool, i, group, pair):
        picks = [pl.multiple_of(index[i, group * GROUP + j] * tile, tile) for j in range(GROUP)]
        return jnp.concatenate([pool[pl.ds(p, tile), pair * 2 * HD : (pair + 1) * 2 * HD] for p in picks], axis=0)

    def score(i, slot):
        for pair in range(heads // 2):
            lanes = [slice((2 * pair + j) * HD, (2 * pair + j + 1) * HD) for j in range(2)]
            query = jnp.concatenate(
                [
                    jnp.concatenate([q_pool[rows_of(i), lanes[0]], zeros], axis=1),
                    jnp.concatenate([zeros, q_pool[rows_of(i), lanes[1]]], axis=1),
                ],
                axis=0,
            )
            top = jnp.full((2 * tile, HD), -jnp.inf, jnp.float32)
            for group in range(groups):
                part = lax.dot_general(
                    query,
                    gathered(k_pool, i, group, pair),
                    (((1,), (1,)), ((), ())),
                    preferred_element_type=jnp.float32,
                )
                place_of = lax.broadcasted_iota(jnp.int32, (1, span), 1) + group * span
                part = jnp.where(place_of < counts[i] * tile, part, -1e30)
                scores[slot, pair, :, group * span : (group + 1) * span] = part
                for j in range(span // HD):
                    top = jnp.maximum(top, part[:, j * HD : (j + 1) * HD])
            tops[slot, pair] = jnp.broadcast_to(jnp.max(top, axis=1, keepdims=True), top.shape)

    def mix(i, slot):
        for pair in range(heads // 2):
            top = tops[slot, pair]
            total = jnp.zeros((2 * tile, HD), jnp.float32)
            mixed = [jnp.zeros((tile, HD), jnp.float32)] * 2
            for group in range(groups):
                rounded = []
                for j in range(span // HD):
                    first = group * span + j * HD
                    weights = jnp.exp2((scores[slot, pair, :, first : first + HD] - top) * factor)
                    total = total + weights
                    rounded.append(weights.astype(jnp.bfloat16))
                both = jnp.dot(
                    jnp.concatenate(rounded, axis=1),
                    gathered(v_pool, i, group, pair),
                    preferred_element_type=jnp.float32,
                )
                mixed = [mixed[0] + both[:tile, :HD], mixed[1] + both[tile:, HD:]]
            total = jnp.sum(total, axis=1, keepdims=True)
            for j in range(2):
                lanes = slice((2 * pair + j) * HD, (2 * pair + j + 1) * HD)
                attended = mixed[j] / total[j * tile : (j + 1) * tile]
                if kept is not None:
                    other = other_pool[rows_of(i), lanes]
                    conditional = jnp.where(side == 0, attended, other)
                    unconditional = jnp.where(side == 0, other, attended)
                    attended = unconditional + guidance_scale * (conditional - unconditional)
                result[rows_of(i), lanes] = attended

    def copy_out(step):
        here = pl.ds(pl.multiple_of(step * 2 * tile, 2 * tile), 2 * tile)
        return pltpu.make_async_copy(result.at[here, :], out.at[here, :], out_sems.at[step])

    for copy in copies[:before_scores]:
        copy.wait()
    score(0, 0)
    for copy in copies[before_scores:]:
        copy.wait()

    def two_tiles(step, carry):
        i = step * 2
        score(i + 1, 1)
        mix(i, 0)
        score(jnp.minimum(i + 2, tiles_here - 1), 0)
        mix(i + 1, 1)
        copy_out(step).start()
        return carry

    lax.fori_loop(0, tiles_here // 2, two_tiles, 0)
    for step in range(tiles_here // 2):
        copy_out(step).wait()


def per_device(queries, keys, values, tile_lists, tile_order):
    queries, keys, values, listed = queries[0], keys[0], values[0], tile_lists[0]
    tiles_here, topk = listed.shape
    rows, features = queries.shape
    tile = rows // tiles_here
    devices = lax.axis_size("seq")
    side, position = lax.axis_index("cfg"), lax.axis_index("seq")
    half = features // 2
    neighbours = len(REACHES)
    chunks = []
    for kept, parts, first in ((False, HANDED, (1 - side) * half), (True, KEPT, side * half)):
        for head, heads in parts:
            chunks.append((kept, head, heads, (first + head * HD).astype(jnp.int32)))

    def buffers(chunk, count):
        width = chunks[chunk][2] * HD
        return [jax.ShapeDtypeStruct((2, CAP * tile, width), keys.dtype)] * count

    def pools(chunk, count):
        width = chunks[chunk][2] * HD
        return [
            pltpu.VMEM((2, rows, width), keys.dtype),
            pltpu.SemaphoreType.DMA((2,)),
            pltpu.SemaphoreType.DMA((2 * count * CAP,)),
        ]

    def first_pack(lists):
        table = jax.ShapeDtypeStruct((neighbours, CAP + 4), jnp.int32)
        return pl.pallas_call(
            functools.partial(first_pack_kernel, tile, tiles_here),
            out_shape=buffers(0, neighbours) + [table],
            in_specs=[SMEM, SMEM] + [VMEM] * neighbours + [ANY, ANY],
            out_specs=[ANY] * neighbours + [SMEM],
            scratch_shapes=[pltpu.SMEM(table.shape, jnp.int32)] + pools(0, neighbours),
            compiler_params=PARAMS,
            cost_estimate=SHORT,
            name="first_pack",
        )(jnp.stack([position, chunks[0][3]]).astype(jnp.int32), tile_order, *lists, keys, values)

    def later_pack(picks, after):
        later = range(1, len(chunks))
        made = pl.pallas_call(
            functools.partial(later_pack_kernel, tile, len(later)),
            out_shape=sum([buffers(chunk, neighbours) for chunk in later], []),
            in_specs=[SMEM, SMEM, ANY, ANY] + [ANY] * len(after),
            out_specs=[ANY] * (neighbours * len(later)),
            scratch_shapes=sum([pools(chunk, neighbours) for chunk in later], []),
            compiler_params=PARAMS,
            cost_estimate=SHORT,
            name="later_pack",
        )(jnp.stack([chunks[chunk][3] for chunk in later]), picks, keys, values, *after)
        return [list(made[i : i + neighbours]) for i in range(0, len(made), neighbours)]

    def moved(sending):
        return [shifted(buffer, "seq", -distance) for buffer, distance in zip(sending, REACHES)]

    counts = jnp.sum((listed >= 0).astype(jnp.int32), axis=1)

    asked = [shifted(listed, "seq", distance) for distance in REACHES]
    *sending, picks = first_pack(asked)
    index = pl.pallas_call(
        functools.partial(index_kernel, tiles_here, devices),
        out_shape=jax.ShapeDtypeStruct(listed.shape, jnp.int32),
        in_specs=[SMEM, SMEM, VMEM],
        out_specs=VMEM,
        compiler_params=PARAMS,
        cost_estimate=SHORT,
        name="pool_index",
    )(position.astype(jnp.int32)[None], tile_order, listed)
    arrived = [moved(sending)]
    arrived += [moved(sending) for sending in later_pack(picks, [arrived[0][2], index])]
    partners, guided, result = [], None, None
    pool = tiles_here * tile + neighbours * CAP * tile
    for chunk, (kept, head, heads, start) in enumerate(chunks):
        width = heads * HD
        operands = [jnp.stack([side, start]).astype(jnp.int32), index, counts, queries, keys, values]
        operands += arrived[chunk]
        aliases, columns = {}, None
        if kept:
            columns = [head * HD]
            for handed_head, handed_heads, partner in partners:
                first, last = max(head, handed_head), min(head + heads, handed_head + handed_heads)
                if first < last:
                    operands.append(partner)
                    columns.append(((first - head) * HD, (first - handed_head) * HD, (last - first) * HD))
        if guided is None and result is not None:
            operands.append(result)
        if guided is not None:
            aliases = {len(operands): 0}
            operands.append(guided)
        out_shape = jax.ShapeDtypeStruct((rows, half if kept else width), jnp.float32)
        result = pl.pallas_call(
            functools.partial(attend_kernel, heads, tile, tiles_here, topk, columns),
            out_shape=out_shape,
            in_specs=[SMEM] * 3 + [ANY] * (len(operands) - 3),
            out_specs=ANY,
            input_output_aliases=aliases,
            scratch_shapes=[
                pltpu.VMEM((rows, width), jnp.bfloat16),
                pltpu.VMEM((pool, width), jnp.bfloat16),
                pltpu.VMEM((pool, width), jnp.bfloat16),
                pltpu.VMEM((2, heads // 2, 2 * tile, topk * tile), jnp.float32),
                pltpu.VMEM((2, heads // 2, 2 * tile, HD), jnp.float32),
                pltpu.VMEM((rows, width), jnp.float32),
                pltpu.VMEM((rows, width) if kept else (8, HD), jnp.float32),
                pltpu.SemaphoreType.DMA((16,)),
                pltpu.SemaphoreType.DMA((tiles_here // 2,)),
            ],
            compiler_params=PARAMS,
            cost_estimate=LONG,
            name=("guide_" if kept else "attend_") + str(chunk),
        )(*operands)
        if kept:
            guided = result
        else:
            partners.append((head, heads, lax.ppermute(result, "cfg", [(0, 1), (1, 0)])))
    return guided


def solution(mesh):
    return jax.shard_map(
        per_device,
        mesh=mesh,
        in_specs=(
            P("cfg", "seq", None),
            P("cfg", "seq", None),
            P("cfg", "seq", None),
            P("cfg", "seq", None),
            P(),
        ),
        out_specs=P("seq", "cfg"),
        check_vma=False,
    )
```

```python
import functools

import jax
import jax.numpy as jnp
from jax import lax
from jax.experimental import pallas as pl
from jax.experimental.pallas import tpu as pltpu
from jax.sharding import PartitionSpec as P

HD = 128
CAP = 4
GROUP = 4
REACHES = (1, -1, 2, -2)
ASKED = (1, 2, -1, -2)
HANDED = ((0, 6), (6, 4))
KEPT = ((0, 6), (6, 4))
guidance_scale = 5.0
ANY = pl.BlockSpec(memory_space=pl.ANY)
SMEM = pl.BlockSpec(memory_space=pltpu.SMEM)
VMEM = pl.BlockSpec(memory_space=pltpu.VMEM)
LONG = pl.CostEstimate(flops=10**13, bytes_accessed=10**11, transcendentals=0)
SHORT = pl.CostEstimate(flops=1, bytes_accessed=1, transcendentals=0)
PARAMS = pltpu.CompilerParams(vmem_limit_bytes=63 * 1024 * 1024)


def shifted(value, axis, steps):
    count = lax.axis_size(axis)
    initial, last = (max(0, -steps), min(count, count - steps))
    return lax.ppermute(value, axis, [(source, source + steps) for source in range(initial, last)])


def any_equal(listed, tile_id):
    return jnp.max((listed == tile_id).astype(jnp.int32))


def pack(tile, start, picks, keys, values, outs, pools, load_sems, sems, plan=None, wait=True):
    width = pools.shape[2]
    columns = pl.ds(pl.multiple_of(start, HD), width)
    loads = [
        pltpu.make_async_copy(source.at[:, columns], pools.at[kind], load_sems.at[kind])
        for kind, source in enumerate((keys, values))
    ]
    for copy in loads:
        copy.start()
    if plan is not None:
        plan()
    copies = []
    for kind in range(2):
        loads[kind].wait()
        for reach in range(len(outs)):
            for entry in range(CAP):
                first = pl.multiple_of(picks[reach, entry] * tile, tile)
                copy = pltpu.make_async_copy(
                    pools.at[kind, pl.ds(first, tile), :],
                    outs[reach].at[kind, pl.ds(entry * tile, tile), :],
                    sems.at[len(copies)],
                )
                copy.start()
                copies.append(copy)
    if wait:
        for copy in copies:
            copy.wait()
    return copies


def first_pack_kernel(tile, tiles_here, place, order, *refs):
    listed = [refs[ASKED.index(distance)] for distance in REACHES]
    keys, values = refs[len(REACHES) : len(REACHES) + 2]
    outs = refs[-5 - len(REACHES) : -5]
    picks_out, picks, pools, load_sems, sems = refs[-5:]
    base = place[0] * tiles_here

    def plan():
        for reach in range(len(REACHES)):
            wanted = listed[reach][...]
            counts = []
            for first in range(0, tiles_here, 6):
                packed = jnp.zeros(wanted.shape, jnp.float32)
                for slot in range(first, first + 6):
                    packed = jnp.where(wanted == order[base + slot], float(16 ** (slot - first)), packed)
                total = jnp.sum(packed).astype(jnp.int32)
                counts += [(total >> (4 * j)) & 15 for j in range(6)]
            filled = jnp.int32(0)
            for entry in range(CAP):
                picks[reach, entry] = 0
            for slot in range(tiles_here):
                picks[reach, filled] = slot
                filled = jnp.minimum(filled + jnp.minimum(counts[slot], 1), CAP)
            for entry in range(CAP):
                picks_out[reach, entry] = picks[reach, entry]

    pack(tile, place[1], picks, keys, values, outs, pools, load_sems, sems, plan)


def later_pack_kernel(tile, count, place, picks, keys, values, *refs):
    outs, scratch = refs[-(len(REACHES) + 3) * count : -3 * count], refs[-3 * count :]
    waits = []
    for chunk in range(count):
        mine = outs[len(REACHES) * chunk : len(REACHES) * (chunk + 1)]
        waits += pack(tile, place[chunk], picks, keys, values, mine, *scratch[3 * chunk : 3 * chunk + 3], wait=False)
    for copy in waits:
        copy.wait()


def index_kernel(tiles_here, devices, place, order, listed_ref, index_ref):
    listed = listed_ref[...]
    here = place[0]
    index = jnp.zeros_like(listed)
    for slot in range(tiles_here):
        index = jnp.where(listed == order[here * tiles_here + slot], slot, index)
    for reach, distance in enumerate(REACHES):
        there = here + distance
        inside = jnp.logical_and(there >= 0, there < devices)
        base = jnp.where(inside, there, here) * tiles_here
        filled = jnp.int32(0)
        for slot in range(tiles_here):
            tile_id = jnp.where(inside, order[base + slot], -2)
            index = jnp.where(listed == tile_id, tiles_here + CAP * reach + filled, index)
            filled = jnp.minimum(filled + any_equal(listed, tile_id), CAP - 1)
    index_ref[...] = index


def attend_kernel(heads, tile, tiles_here, topk, kept, place, index, counts, queries, keys, values, *refs):
    arrived = refs[: len(REACHES)]
    rest = refs[len(REACHES) :]
    out, q_pool, k_pool, v_pool, scores, tops, result, other_pool, in_sems, out_sems = rest[-10:]
    rows = tile * tiles_here
    units = [(first, min(2, heads - first)) for first in range(0, heads, 2)]
    if kept is not None:
        out = out.at[:, pl.ds(kept[0], heads * HD)]
    factor = HD ** (-0.5) * 1.4426950408889634
    side = place[0]
    span = GROUP * tile
    groups = topk // GROUP
    zeros = jnp.zeros((tile, HD), jnp.bfloat16)
    sems_each = 4 + 2 * len(REACHES)

    def lanes_of(unit):
        first, count = units[unit]
        return slice(first * HD, (first + count) * HD)

    loads = []
    for unit, (first, count) in enumerate(units):
        here = pl.ds(first * HD, count * HD)
        own = pl.ds(pl.multiple_of(place[1] + first * HD, HD), count * HD)
        pairs = [(queries.at[:, own], q_pool.at[:, here])]
        for kind, (source, pool) in enumerate(((keys, k_pool), (values, v_pool))):
            pairs.append((source.at[:, own], pool.at[pl.ds(0, rows), here]))
            for reach in range(len(REACHES)):
                remote = pl.ds(rows + reach * CAP * tile, CAP * tile)
                pairs.append((arrived[reach].at[kind, :, here], pool.at[remote, here]))
        if kept is not None:
            for piece, (to, source, wide) in enumerate(kept[1:]):
                start, end = max(to, first * HD), min(to + wide, (first + count) * HD)
                if start < end:
                    taken = rest[piece].at[:, pl.ds(source + start - to, end - start)]
                    pairs.append((taken, other_pool.at[:, pl.ds(start, end - start)]))
        loads.append(
            [pltpu.make_async_copy(*pair, in_sems.at[unit * sems_each + i]) for i, pair in enumerate(pairs)]
        )
    for copies in loads:
        for copy in copies:
            copy.start()

    def rows_of(i):
        return pl.ds(pl.multiple_of(i * tile, tile), tile)

    def gathered(pool, i, group, unit):
        picks = [pl.multiple_of(index[i, group * GROUP + j] * tile, tile) for j in range(GROUP)]
        return jnp.concatenate([pool[pl.ds(p, tile), lanes_of(unit)] for p in picks], axis=0)

    def score(unit, stage):
        first, count = units[unit]
        for k in range(2):
            i = 2 * stage + k
            query = q_pool[rows_of(i), lanes_of(unit)]
            if count == 2:
                query = jnp.concatenate(
                    [
                        jnp.concatenate([query[:, :HD], zeros], axis=1),
                        jnp.concatenate([zeros, query[:, HD:]], axis=1),
                    ],
                    axis=0,
                )
            top = jnp.full((count * tile, HD), -jnp.inf, jnp.float32)
            for group in range(groups):
                part = lax.dot_general(
                    query,
                    gathered(k_pool, i, group, unit),
                    (((1,), (1,)), ((), ())),
                    preferred_element_type=jnp.float32,
                )
                place_of = lax.broadcasted_iota(jnp.int32, (1, span), 1) + group * span
                part = jnp.where(place_of < counts[i] * tile, part, -1e30)
                scores[stage % 2, k, : count * tile, group * span : (group + 1) * span] = part
                for j in range(span // HD):
                    top = jnp.maximum(top, part[:, j * HD : (j + 1) * HD])
            tops[stage % 2, k, : count * tile] = jnp.broadcast_to(jnp.max(top, axis=1, keepdims=True), top.shape)

    def mix(unit, stage):
        first, count = units[unit]
        for k in range(2):
            i = 2 * stage + k
            top = tops[stage % 2, k, : count * tile]
            total = jnp.zeros((count * tile, HD), jnp.float32)
            mixed = [jnp.zeros((tile, HD), jnp.float32)] * count
            for group in range(groups):
                rounded = []
                for j in range(span // HD):
                    at = group * span + j * HD
                    weights = jnp.exp2((scores[stage % 2, k, : count * tile, at : at + HD] - top) * factor)
                    total = total + weights
                    rounded.append(weights.astype(jnp.bfloat16))
                both = jnp.dot(
                    jnp.concatenate(rounded, axis=1),
                    gathered(v_pool, i, group, unit),
                    preferred_element_type=jnp.float32,
                )
                mixed = [mixed[j] + both[j * tile : (j + 1) * tile, j * HD : (j + 1) * HD] for j in range(count)]
            total = jnp.sum(total, axis=1, keepdims=True)
            for j in range(count):
                lanes = slice((first + j) * HD, (first + j + 1) * HD)
                attended = mixed[j] / total[j * tile : (j + 1) * tile]
                if kept is not None:
                    other = other_pool[rows_of(i), lanes]
                    conditional = jnp.where(side == 0, attended, other)
                    unconditional = jnp.where(side == 0, other, attended)
                    attended = unconditional + guidance_scale * (conditional - unconditional)
                result[rows_of(i), lanes] = attended

    class Stage:
        def __init__(self, base, parity):
            self.base, self.parity = base, parity

        def __rmul__(self, other):
            return other * (self.base + self.parity)

        def __mod__(self, other):
            return self.parity

    def copy_out(unit, half):
        here = pl.ds(half * rows // 2, rows // 2)
        lanes = pl.ds(units[unit][0] * HD, units[unit][1] * HD)
        return pltpu.make_async_copy(result.at[here, lanes], out.at[here, lanes], out_sems.at[2 * unit + half])

    stages = tiles_here // 2
    for copy in loads[0][: 2 + len(REACHES)]:
        copy.wait()
    score(0, 0)
    for unit in range(len(units)):
        for copy in loads[unit][2 + len(REACHES) :]:
            copy.wait()

        def two_stages(step, carry, unit=unit):
            base = step * 2
            score(unit, Stage(base, 1))
            mix(unit, Stage(base, 0))
            score(unit, Stage(base + 2, 0))
            mix(unit, Stage(base, 1))
            return carry

        lax.fori_loop(0, (stages - 1) // 2, two_stages, 0)
        copy_out(unit, 0).start()
        score(unit, stages - 1)
        mix(unit, stages - 2)
        if unit + 1 < len(units):
            for copy in loads[unit + 1][: 2 + len(REACHES)]:
                copy.wait()
            score(unit + 1, 0)
        mix(unit, stages - 1)
        copy_out(unit, 1).start()
    for unit in range(len(units)):
        for half in range(2):
            copy_out(unit, half).wait()


def per_device(queries, keys, values, tile_lists, tile_order):
    queries, keys, values, listed = queries[0], keys[0], values[0], tile_lists[0]
    tiles_here, topk = listed.shape
    rows, features = queries.shape
    tile = rows // tiles_here
    devices = lax.axis_size("seq")
    side, position = lax.axis_index("cfg"), lax.axis_index("seq")
    half = features // 2
    neighbours = len(REACHES)
    chunks = []
    for kept, parts, first in ((False, HANDED, (1 - side) * half), (True, KEPT, side * half)):
        for head, heads in parts:
            chunks.append((kept, head, heads, (first + head * HD).astype(jnp.int32)))

    def buffers(chunk, count):
        width = chunks[chunk][2] * HD
        return [jax.ShapeDtypeStruct((2, CAP * tile, width), keys.dtype)] * count

    def pools(chunk, count):
        width = chunks[chunk][2] * HD
        return [
            pltpu.VMEM((2, rows, width), keys.dtype),
            pltpu.SemaphoreType.DMA((2,)),
            pltpu.SemaphoreType.DMA((2 * count * CAP,)),
        ]

    def first_pack(lists):
        table = jax.ShapeDtypeStruct((neighbours, CAP + 4), jnp.int32)
        return pl.pallas_call(
            functools.partial(first_pack_kernel, tile, tiles_here),
            out_shape=buffers(0, neighbours) + [table],
            in_specs=[SMEM, SMEM] + [VMEM] * neighbours + [ANY, ANY],
            out_specs=[ANY] * neighbours + [SMEM],
            scratch_shapes=[pltpu.SMEM(table.shape, jnp.int32)] + pools(0, neighbours),
            compiler_params=PARAMS,
            cost_estimate=SHORT,
            name="first_pack",
        )(jnp.stack([position, chunks[0][3]]).astype(jnp.int32), tile_order, *lists, keys, values)

    def later_pack(picks, after):
        later = range(1, len(chunks))
        made = pl.pallas_call(
            functools.partial(later_pack_kernel, tile, len(later)),
            out_shape=sum([buffers(chunk, neighbours) for chunk in later], []),
            in_specs=[SMEM, SMEM, ANY, ANY] + [ANY] * len(after),
            out_specs=[ANY] * (neighbours * len(later)),
            scratch_shapes=sum([pools(chunk, neighbours) for chunk in later], []),
            compiler_params=PARAMS,
            cost_estimate=SHORT,
            name="later_pack",
        )(jnp.stack([chunks[chunk][3] for chunk in later]), picks, keys, values, *after)
        return [list(made[i : i + neighbours]) for i in range(0, len(made), neighbours)]

    def moved(sending):
        return [shifted(buffer, "seq", -distance) for buffer, distance in zip(sending, REACHES)]

    counts = jnp.sum((listed >= 0).astype(jnp.int32), axis=1)

    asked = [shifted(listed, "seq", distance) for distance in ASKED]
    *sending, picks = first_pack(asked)
    index = pl.pallas_call(
        functools.partial(index_kernel, tiles_here, devices),
        out_shape=jax.ShapeDtypeStruct(listed.shape, jnp.int32),
        in_specs=[SMEM, SMEM, VMEM],
        out_specs=VMEM,
        compiler_params=PARAMS,
        cost_estimate=SHORT,
        name="pool_index",
    )(position.astype(jnp.int32)[None], tile_order, listed)
    arrived = [moved(sending)]
    arrived += [moved(sending) for sending in later_pack(picks, [arrived[0][2], index])]
    partners, guided, result = [], None, None
    pool = tiles_here * tile + neighbours * CAP * tile
    for chunk, (kept, head, heads, start) in enumerate(chunks):
        width = heads * HD
        operands = [jnp.stack([side, start]).astype(jnp.int32), index, counts, queries, keys, values]
        operands += arrived[chunk]
        aliases, columns = {}, None
        if kept:
            columns = [head * HD]
            for handed_head, handed_heads, partner in partners:
                first, last = max(head, handed_head), min(head + heads, handed_head + handed_heads)
                if first < last:
                    operands.append(partner)
                    columns.append(((first - head) * HD, (first - handed_head) * HD, (last - first) * HD))
        if guided is None and result is not None:
            operands.append(result)
        if guided is not None:
            aliases = {len(operands): 0}
            operands.append(guided)
        out_shape = jax.ShapeDtypeStruct((rows, half if kept else width), jnp.float32)
        result = pl.pallas_call(
            functools.partial(attend_kernel, heads, tile, tiles_here, topk, columns),
            out_shape=out_shape,
            in_specs=[SMEM] * 3 + [ANY] * (len(operands) - 3),
            out_specs=ANY,
            input_output_aliases=aliases,
            scratch_shapes=[
                pltpu.VMEM((rows, width), jnp.bfloat16),
                pltpu.VMEM((pool, width), jnp.bfloat16),
                pltpu.VMEM((pool, width), jnp.bfloat16),
                pltpu.VMEM((2, 2, 2 * tile, topk * tile), jnp.float32),
                pltpu.VMEM((2, 2, 2 * tile, HD), jnp.float32),
                pltpu.VMEM((rows, width), jnp.float32),
                pltpu.VMEM((rows, width) if kept else (8, HD), jnp.float32),
                pltpu.SemaphoreType.DMA(((heads + 1) // 2 * (4 + 2 * neighbours),)),
                pltpu.SemaphoreType.DMA((heads + heads % 2,)),
            ],
            compiler_params=PARAMS,
            cost_estimate=LONG,
            name=("guide_" if kept else "attend_") + str(chunk),
        )(*operands)
        if kept:
            guided = result
        else:
            partners.append((head, heads, lax.ppermute(result, "cfg", [(0, 1), (1, 0)])))
    return guided


def solution(mesh):
    return jax.shard_map(
        per_device,
        mesh=mesh,
        in_specs=(
            P("cfg", "seq", None),
            P("cfg", "seq", None),
            P("cfg", "seq", None),
            P("cfg", "seq", None),
            P(),
        ),
        out_specs=P("seq", "cfg"),
        check_vma=False,
    )
```

```python
import functools

import jax
import jax.numpy as jnp
from jax import lax
from jax.experimental import pallas as pl
from jax.experimental.pallas import tpu as pltpu
from jax.sharding import PartitionSpec as P

HD = 128
CAP = 4
GROUP = 4
REACHES = (1, 2, -1, -2)
ASKED = (1, 2, -1, -2)
HANDED = ((0, 6), (6, 4))
KEPT = ((0, 6), (6, 4))
guidance_scale = 5.0
ANY = pl.BlockSpec(memory_space=pl.ANY)
SMEM = pl.BlockSpec(memory_space=pltpu.SMEM)
VMEM = pl.BlockSpec(memory_space=pltpu.VMEM)
LONG = pl.CostEstimate(flops=10**13, bytes_accessed=10**11, transcendentals=0)
SHORT = pl.CostEstimate(flops=1, bytes_accessed=1, transcendentals=0)
PARAMS = pltpu.CompilerParams(vmem_limit_bytes=63 * 1024 * 1024)


def shifted(value, axis, steps):
    count = lax.axis_size(axis)
    initial, last = (max(0, -steps), min(count, count - steps))
    return lax.ppermute(value, axis, [(source, source + steps) for source in range(initial, last)])


def any_equal(listed, tile_id):
    return jnp.max((listed == tile_id).astype(jnp.int32))


def pack(tile, start, picks, keys, values, outs, pools, load_sems, sems, plan=None, wait=True):
    width = pools.shape[2]
    columns = pl.ds(pl.multiple_of(start, HD), width)
    loads = [
        pltpu.make_async_copy(source.at[:, columns], pools.at[kind], load_sems.at[kind])
        for kind, source in enumerate((keys, values))
    ]
    for copy in loads:
        copy.start()
    if plan is not None:
        plan()
    copies = []
    for kind in range(2):
        loads[kind].wait()
        for reach in range(len(outs)):
            for entry in range(CAP):
                first = pl.multiple_of(picks[reach, entry] * tile, tile)
                copy = pltpu.make_async_copy(
                    pools.at[kind, pl.ds(first, tile), :],
                    outs[reach].at[kind, pl.ds(entry * tile, tile), :],
                    sems.at[len(copies)],
                )
                copy.start()
                copies.append(copy)
    if wait:
        for copy in copies:
            copy.wait()
    return copies


def first_pack_kernel(tile, tiles_here, place, order, *refs):
    listed = [refs[ASKED.index(distance)] for distance in REACHES]
    keys, values = refs[len(REACHES) : len(REACHES) + 2]
    outs = refs[-5 - len(REACHES) : -5]
    picks_out, picks, pools, load_sems, sems = refs[-5:]
    base = place[0] * tiles_here

    def plan():
        for reach in range(len(REACHES)):
            wanted = listed[reach][...]
            counts = []
            for first in range(0, tiles_here, 6):
                packed = jnp.zeros(wanted.shape, jnp.float32)
                for slot in range(first, first + 6):
                    packed = jnp.where(wanted == order[base + slot], float(16 ** (slot - first)), packed)
                total = jnp.sum(packed).astype(jnp.int32)
                counts += [(total >> (4 * j)) & 15 for j in range(6)]
            filled = jnp.int32(0)
            for entry in range(CAP):
                picks[reach, entry] = 0
            for slot in range(tiles_here):
                picks[reach, filled] = slot
                filled = jnp.minimum(filled + jnp.minimum(counts[slot], 1), CAP)
            for entry in range(CAP):
                picks_out[reach, entry] = picks[reach, entry]

    pack(tile, place[1], picks, keys, values, outs, pools, load_sems, sems, plan)


def later_pack_kernel(tile, count, place, picks, keys, values, *refs):
    outs, scratch = refs[-(len(REACHES) + 3) * count : -3 * count], refs[-3 * count :]
    waits = []
    for chunk in range(count):
        mine = outs[len(REACHES) * chunk : len(REACHES) * (chunk + 1)]
        waits += pack(tile, place[chunk], picks, keys, values, mine, *scratch[3 * chunk : 3 * chunk + 3], wait=False)
    for copy in waits:
        copy.wait()


def index_kernel(tiles_here, devices, place, order, listed_ref, index_ref):
    listed = listed_ref[...]
    here = place[0]
    index = jnp.zeros_like(listed)
    for slot in range(tiles_here):
        index = jnp.where(listed == order[here * tiles_here + slot], slot, index)
    for reach, distance in enumerate(REACHES):
        there = here + distance
        inside = jnp.logical_and(there >= 0, there < devices)
        base = jnp.where(inside, there, here) * tiles_here
        filled = jnp.int32(0)
        for slot in range(tiles_here):
            tile_id = jnp.where(inside, order[base + slot], -2)
            index = jnp.where(listed == tile_id, tiles_here + CAP * reach + filled, index)
            filled = jnp.minimum(filled + any_equal(listed, tile_id), CAP - 1)
    index_ref[...] = index


def attend_kernel(heads, tile, tiles_here, topk, kept, place, index, counts, queries, keys, values, *refs):
    arrived = refs[: len(REACHES)]
    rest = refs[len(REACHES) :]
    out, q_pool, k_pool, v_pool, scores, tops, result, other_pool, in_sems, out_sems = rest[-10:]
    rows = tile * tiles_here
    units = [(first, min(2, heads - first)) for first in range(0, heads, 2)]
    if kept is not None:
        out = out.at[:, pl.ds(kept[0], heads * HD)]
    factor = HD ** (-0.5) * 1.4426950408889634
    side = place[0]
    span = GROUP * tile
    groups = topk // GROUP
    zeros = jnp.zeros((tile, HD), jnp.bfloat16)
    sems_each = 4 + 2 * len(REACHES)

    def lanes_of(unit):
        first, count = units[unit]
        return slice(first * HD, (first + count) * HD)

    loads = []
    for unit, (first, count) in enumerate(units):
        here = pl.ds(first * HD, count * HD)
        own = pl.ds(pl.multiple_of(place[1] + first * HD, HD), count * HD)
        pairs = [(queries.at[:, own], q_pool.at[:, here])]
        for kind, (source, pool) in enumerate(((keys, k_pool), (values, v_pool))):
            pairs.append((source.at[:, own], pool.at[pl.ds(0, rows), here]))
            for reach in range(len(REACHES)):
                remote = pl.ds(rows + reach * CAP * tile, CAP * tile)
                pairs.append((arrived[reach].at[kind, :, here], pool.at[remote, here]))
        if kept is not None:
            for piece, (to, source, wide) in enumerate(kept[1:]):
                start, end = max(to, first * HD), min(to + wide, (first + count) * HD)
                if start < end:
                    taken = rest[piece].at[:, pl.ds(source + start - to, end - start)]
                    pairs.append((taken, other_pool.at[:, pl.ds(start, end - start)]))
        loads.append(
            [pltpu.make_async_copy(*pair, in_sems.at[unit * sems_each + i]) for i, pair in enumerate(pairs)]
        )
    for copies in loads:
        for copy in copies:
            copy.start()

    def rows_of(i):
        return pl.ds(pl.multiple_of(i * tile, tile), tile)

    def gathered(pool, i, group, unit):
        picks = [pl.multiple_of(index[i, group * GROUP + j] * tile, tile) for j in range(GROUP)]
        return jnp.concatenate([pool[pl.ds(p, tile), lanes_of(unit)] for p in picks], axis=0)

    def score(unit, stage):
        first, count = units[unit]
        for k in range(2):
            i = 2 * stage + k
            query = q_pool[rows_of(i), lanes_of(unit)]
            if count == 2:
                query = jnp.concatenate(
                    [
                        jnp.concatenate([query[:, :HD], zeros], axis=1),
                        jnp.concatenate([zeros, query[:, HD:]], axis=1),
                    ],
                    axis=0,
                )
            top = jnp.full((count * tile, HD), -jnp.inf, jnp.float32)
            for group in range(groups):
                part = lax.dot_general(
                    query,
                    gathered(k_pool, i, group, unit),
                    (((1,), (1,)), ((), ())),
                    preferred_element_type=jnp.float32,
                )
                place_of = lax.broadcasted_iota(jnp.int32, (1, span), 1) + group * span
                part = jnp.where(place_of < counts[i] * tile, part, -1e30)
                scores[stage % 2, k, : count * tile, group * span : (group + 1) * span] = part
                for j in range(span // HD):
                    top = jnp.maximum(top, part[:, j * HD : (j + 1) * HD])
            tops[stage % 2, k, : count * tile] = jnp.broadcast_to(jnp.max(top, axis=1, keepdims=True), top.shape)

    def mix(unit, stage):
        first, count = units[unit]
        for k in range(2):
            i = 2 * stage + k
            top = tops[stage % 2, k, : count * tile]
            total = jnp.zeros((count * tile, HD), jnp.float32)
            mixed = [jnp.zeros((tile, HD), jnp.float32)] * count
            for group in range(groups):
                rounded = []
                for j in range(span // HD):
                    at = group * span + j * HD
                    weights = jnp.exp2((scores[stage % 2, k, : count * tile, at : at + HD] - top) * factor)
                    total = total + weights
                    rounded.append(weights.astype(jnp.bfloat16))
                both = jnp.dot(
                    jnp.concatenate(rounded, axis=1),
                    gathered(v_pool, i, group, unit),
                    preferred_element_type=jnp.float32,
                )
                mixed = [mixed[j] + both[j * tile : (j + 1) * tile, j * HD : (j + 1) * HD] for j in range(count)]
            total = jnp.sum(total, axis=1, keepdims=True)
            for j in range(count):
                lanes = slice((first + j) * HD, (first + j + 1) * HD)
                attended = mixed[j] / total[j * tile : (j + 1) * tile]
                if kept is not None:
                    other = other_pool[rows_of(i), lanes]
                    conditional = jnp.where(side == 0, attended, other)
                    unconditional = jnp.where(side == 0, other, attended)
                    attended = unconditional + guidance_scale * (conditional - unconditional)
                result[rows_of(i), lanes] = attended

    class Stage:
        def __init__(self, base, parity):
            self.base, self.parity = base, parity

        def __rmul__(self, other):
            return other * (self.base + self.parity)

        def __mod__(self, other):
            return self.parity

    def copy_out(unit, half):
        here = pl.ds(half * rows // 2, rows // 2)
        lanes = pl.ds(units[unit][0] * HD, units[unit][1] * HD)
        return pltpu.make_async_copy(result.at[here, lanes], out.at[here, lanes], out_sems.at[2 * unit + half])

    stages = tiles_here // 2
    for copy in loads[0][: 2 + len(REACHES)]:
        copy.wait()
    score(0, 0)
    for unit in range(len(units)):
        for copy in loads[unit][2 + len(REACHES) :]:
            copy.wait()

        def two_stages(step, carry, unit=unit):
            base = step * 2
            score(unit, Stage(base, 1))
            mix(unit, Stage(base, 0))
            score(unit, Stage(base + 2, 0))
            mix(unit, Stage(base, 1))
            return carry

        lax.fori_loop(0, (stages - 1) // 2, two_stages, 0)
        copy_out(unit, 0).start()
        score(unit, stages - 1)
        mix(unit, stages - 2)
        if unit + 1 < len(units):
            for copy in loads[unit + 1][: 2 + len(REACHES)]:
                copy.wait()
            score(unit + 1, 0)
        mix(unit, stages - 1)
        copy_out(unit, 1).start()
    for unit in range(len(units)):
        for half in range(2):
            copy_out(unit, half).wait()


def per_device(queries, keys, values, tile_lists, tile_order):
    queries, keys, values, listed = queries[0], keys[0], values[0], tile_lists[0]
    tiles_here, topk = listed.shape
    rows, features = queries.shape
    tile = rows // tiles_here
    devices = lax.axis_size("seq")
    side, position = lax.axis_index("cfg"), lax.axis_index("seq")
    half = features // 2
    neighbours = len(REACHES)
    chunks = []
    for kept, parts, first in ((False, HANDED, (1 - side) * half), (True, KEPT, side * half)):
        for head, heads in parts:
            chunks.append((kept, head, heads, (first + head * HD).astype(jnp.int32)))

    def buffers(chunk, count):
        width = chunks[chunk][2] * HD
        return [jax.ShapeDtypeStruct((2, CAP * tile, width), keys.dtype)] * count

    def pools(chunk, count):
        width = chunks[chunk][2] * HD
        return [
            pltpu.VMEM((2, rows, width), keys.dtype),
            pltpu.SemaphoreType.DMA((2,)),
            pltpu.SemaphoreType.DMA((2 * count * CAP,)),
        ]

    def first_pack(lists):
        table = jax.ShapeDtypeStruct((neighbours, CAP + 4), jnp.int32)
        return pl.pallas_call(
            functools.partial(first_pack_kernel, tile, tiles_here),
            out_shape=buffers(0, neighbours) + [table],
            in_specs=[SMEM, SMEM] + [VMEM] * neighbours + [ANY, ANY],
            out_specs=[ANY] * neighbours + [SMEM],
            scratch_shapes=[pltpu.SMEM(table.shape, jnp.int32)] + pools(0, neighbours),
            compiler_params=PARAMS,
            cost_estimate=SHORT,
            name="first_pack",
        )(jnp.stack([position, chunks[0][3]]).astype(jnp.int32), tile_order, *lists, keys, values)

    def later_pack(picks, after):
        later = range(1, len(chunks))
        made = pl.pallas_call(
            functools.partial(later_pack_kernel, tile, len(later)),
            out_shape=sum([buffers(chunk, neighbours) for chunk in later], []),
            in_specs=[SMEM, SMEM, ANY, ANY] + [ANY] * len(after),
            out_specs=[ANY] * (neighbours * len(later)),
            scratch_shapes=sum([pools(chunk, neighbours) for chunk in later], []),
            compiler_params=PARAMS,
            cost_estimate=SHORT,
            name="later_pack",
        )(jnp.stack([chunks[chunk][3] for chunk in later]), picks, keys, values, *after)
        return [list(made[i : i + neighbours]) for i in range(0, len(made), neighbours)]

    def moved(sending):
        return [shifted(buffer, "seq", -distance) for buffer, distance in zip(sending, REACHES)]

    counts = jnp.sum((listed >= 0).astype(jnp.int32), axis=1)

    asked = [shifted(listed, "seq", distance) for distance in ASKED]
    *sending, picks = first_pack(asked)
    index = pl.pallas_call(
        functools.partial(index_kernel, tiles_here, devices),
        out_shape=jax.ShapeDtypeStruct(listed.shape, jnp.int32),
        in_specs=[SMEM, SMEM, VMEM],
        out_specs=VMEM,
        compiler_params=PARAMS,
        cost_estimate=SHORT,
        name="pool_index",
    )(position.astype(jnp.int32)[None], tile_order, listed)
    arrived = [moved(sending)]
    arrived += [moved(sending) for sending in later_pack(picks, [arrived[0][REACHES.index(2)], index])]
    partners, guided, result = [], None, None
    pool = tiles_here * tile + neighbours * CAP * tile
    for chunk, (kept, head, heads, start) in enumerate(chunks):
        width = heads * HD
        operands = [jnp.stack([side, start]).astype(jnp.int32), index, counts, queries, keys, values]
        operands += arrived[chunk]
        aliases, columns = {}, None
        if kept:
            columns = [head * HD]
            for handed_head, handed_heads, partner in partners:
                first, last = max(head, handed_head), min(head + heads, handed_head + handed_heads)
                if first < last:
                    operands.append(partner)
                    columns.append(((first - head) * HD, (first - handed_head) * HD, (last - first) * HD))
        if guided is None and result is not None:
            operands.append(result)
        if guided is not None:
            aliases = {len(operands): 0}
            operands.append(guided)
        out_shape = jax.ShapeDtypeStruct((rows, half if kept else width), jnp.float32)
        result = pl.pallas_call(
            functools.partial(attend_kernel, heads, tile, tiles_here, topk, columns),
            out_shape=out_shape,
            in_specs=[SMEM] * 3 + [ANY] * (len(operands) - 3),
            out_specs=ANY,
            input_output_aliases=aliases,
            scratch_shapes=[
                pltpu.VMEM((rows, width), jnp.bfloat16),
                pltpu.VMEM((pool, width), jnp.bfloat16),
                pltpu.VMEM((pool, width), jnp.bfloat16),
                pltpu.VMEM((2, 2, 2 * tile, topk * tile), jnp.float32),
                pltpu.VMEM((2, 2, 2 * tile, HD), jnp.float32),
                pltpu.VMEM((rows, width), jnp.float32),
                pltpu.VMEM((rows, width) if kept else (8, HD), jnp.float32),
                pltpu.SemaphoreType.DMA(((heads + 1) // 2 * (4 + 2 * neighbours),)),
                pltpu.SemaphoreType.DMA((heads + heads % 2,)),
            ],
            compiler_params=PARAMS,
            cost_estimate=LONG,
            name=("guide_" if kept else "attend_") + str(chunk),
        )(*operands)
        if kept:
            guided = result
        else:
            partners.append((head, heads, lax.ppermute(result, "cfg", [(0, 1), (1, 0)])))
    return guided


def solution(mesh):
    return jax.shard_map(
        per_device,
        mesh=mesh,
        in_specs=(
            P("cfg", "seq", None),
            P("cfg", "seq", None),
            P("cfg", "seq", None),
            P("cfg", "seq", None),
            P(),
        ),
        out_specs=P("seq", "cfg"),
        check_vma=False,
    )
```
